32 devices in a mesh: ta: 4 (over x, core), sa: 8 (over z, y).
Axes of the slice: x: 2, y: 2, z: 4, core: 2. Of those that a mesh axis runs over, the one named last changes fastest.
Arguments:
- video: bfloat16 [32, 8, 128, 1024], P('ta', 'sa'), may hold values from -6 to 6
- mix_gain: float32 [1024], replicated, may hold values from 0.1 to 1.9
- t_rate: float32 [1024], replicated, may hold values from 0.02 to 2
- s_kernel: float32 [15, 1024], replicated, may hold values from -2 to 2
- w_gate: bfloat16 [1024, 1024], replicated, may hold values from -0.1875 to 0.1875
- w_up: bfloat16 [1024, 1024], replicated, may hold values from -0.1875 to 0.1875
- w_down: bfloat16 [1024, 1024], replicated, may hold values from -0.1875 to 0.1875
Outputs:
- result: bfloat16 [32, 8, 128, 1024], P('ta', 'sa')
The draws below stay inside these ranges and needn't reach their ends.
All inputs are finite; a program needn't handle non-finite values.
Results may differ from the reference program's by a relative error of at most 0.0063.
Values may be sent and summed in bfloat16 or wider, within the bound.
A program may use at most 128 MiB of HBM per device.

```python
import math
import jax
import jax.numpy as jnp
from jax import lax

C = 1024
HID = 1024
FB = 8
W = 128
F = 32
H = 8


def shard_levels(rng, shape, pieces, low, largest):
    def one(axis_at, blocks):
        draws = jax.random.uniform(jax.random.fold_in(jax.random.fold_in(rng, 6), axis_at), (blocks,), jnp.float32, low / len(pieces), largest / len(pieces))
        return jnp.repeat(jnp.exp(draws), shape[axis_at] // blocks).reshape((-1,) + (1,) * (len(shape) - axis_at - 1))

    level = one(*pieces[0])
    for cut in pieces[1:]:
        level = level * one(*cut)
    return level


def bell_draw(rng, shape, spread, bound, shards=(), kind=jnp.bfloat16):
    values = spread * jax.random.normal(rng, shape, jnp.float32)
    if shards:
        values = values * shard_levels(rng, shape, shards, -0.22, 0.18)
    return jnp.clip(values, -bound, bound).astype(kind)


def setup_inputs(seed: int = 0) -> dict:
    seeds = jax.random.split(jax.random.key(seed), 8)
    return {
        "video": bell_draw(seeds[0], (F, H, W, C), 1.0, 6.0, ((0, 4), (1, 8))),
        "mix_gain": jnp.clip(1.0 + 0.18 * jax.random.normal(seeds[1], (C,), jnp.float32), 0.1, 1.9),
        "t_rate": jnp.clip(jnp.exp(jax.random.uniform(seeds[2], (C,), jnp.float32, math.log(0.02), math.log(2.0))), 0.02, 2.0),
        "s_kernel": bell_draw(seeds[3], (2 * H - 1, C), H ** -0.5, 2.0, (), jnp.float32),
        "w_gate": bell_draw(seeds[4], (C, HID), C ** -0.5, 0.1875),
        "w_up": bell_draw(seeds[5], (C, HID), C ** -0.5, 0.1875),
        "w_down": bell_draw(seeds[6], (HID, C), HID ** -0.5, 0.1875),
    }


epsilon = 1e-06

def reference(video, mix_gain, t_rate, s_kernel, w_gate, w_up, w_down):
    widened_in = video.astype(jnp.float32)
    normed = (widened_in * lax.rsqrt(lax.optimization_barrier(jnp.mean(widened_in * widened_in, -1, keepdims=True)) + epsilon)).astype(jnp.bfloat16)
    offsets = jnp.arange(-FB, FB + 1)
    kernel_taps = jnp.exp(-t_rate[None, :] * jnp.abs(offsets).astype(jnp.float32)[:, None])
    padded = jnp.pad(normed, ((FB, FB), (0, 0), (0, 0), (0, 0)))
    temporal_mix = jnp.zeros(normed.shape, jnp.float32)
    for tap_index in range(2 * FB + 1):
        shift_by = tap_index - FB
        temporal_mix = temporal_mix + kernel_taps[tap_index] * padded[FB - shift_by:FB - shift_by + F].astype(jnp.float32)
    row_ids = jnp.arange(H)
    offset_idx = row_ids[:, None] - row_ids[None, :] + H - 1
    toeplitz = jnp.take(s_kernel, offset_idx, axis=0)

    def one_frame(frame_args):
        normed_frame, temporal_frame, video_frame = frame_args
        spatial_mix = jnp.einsum('hkc,kwc->hwc', toeplitz, normed_frame.astype(jnp.float32), precision=lax.Precision.HIGHEST)
        summed = (temporal_frame + spatial_mix).astype(jnp.bfloat16)
        widened = lax.optimization_barrier(summed).astype(jnp.float32)
        normal_mix = (widened * lax.rsqrt(lax.optimization_barrier(jnp.mean(widened * widened, -1, keepdims=True)) + epsilon) * mix_gain).astype(jnp.bfloat16)
        flat_rows = normal_mix.reshape(-1, C)
        gate_act = jnp.dot(flat_rows, w_gate, preferred_element_type=jnp.float32)
        up_act = jnp.dot(flat_rows, w_up, preferred_element_type=jnp.float32)
        hidden = (jax.nn.silu(gate_act) * up_act).astype(jnp.bfloat16)
        output = video_frame.reshape(-1, C).astype(jnp.float32) + jnp.dot(hidden, w_down, preferred_element_type=jnp.float32)
        return output.astype(jnp.bfloat16).reshape(video_frame.shape)
    return lax.map(one_frame, (normed, temporal_mix, video))
```

```python
import functools

import jax
import jax.numpy as jnp
from jax import lax
from jax.experimental import pallas as pl
from jax.experimental.pallas import tpu as pltpu
from jax.sharding import PartitionSpec as P

EPS = 1e-06
MESH = pl.DeviceIdType.MESH
ROWS = 16
LANES = 128
COLS = 256
F32 = jnp.float32
BF16 = jnp.bfloat16


def loop(start, stop, step_fn):
    def step(i, carry):
        step_fn(i)
        return carry

    lax.fori_loop(start, stop, step, 0)


def aligned(index, size):
    return pl.ds(pl.multiple_of(index * size, size), size)


def kernel(
    n, nt, chunks,
    video_hbm, gain_ref, rate_ref, taps_ref, gate_hbm, up_hbm, down_hbm,
    out_hbm,
    video, normed, prev, after, got, mixed, back, time_mix, normal, hidden, out,
    w_gate, w_up, w_down, decay,
    load_sem, weight_sem, store_sem,
    fwd_send, fwd_recv, back_send, back_recv, halo_send, halo_recv,
):
    frames, width, channels = video.shape
    group = frames * width // n
    part = group // chunks
    cols = width // chunks
    me = lax.axis_index("sa")
    t = lax.axis_index("ta")
    per_frame = width // group
    tiles = channels // LANES

    def chunk_cols(c):
        return pl.ds(c * cols, cols)

    def place(p, c):
        start = lax.rem(p, per_frame) * group + c * part
        return p // per_frame, pl.ds(pl.multiple_of(start, part), part)

    loads = []
    for c in range(chunks):
        load = pltpu.make_async_copy(
            video_hbm.at[:, chunk_cols(c)], video.at[:, chunk_cols(c)], load_sem.at[c]
        )
        load.start()
        loads.append(load)

    barrier = pltpu.get_barrier_semaphore()

    def greet(o):
        pl.semaphore_signal(
            barrier, inc=1, device_id={"sa": lax.rem(me + o, n)}, device_id_type=MESH
        )

    loop(1, n, greet)

    @pl.when(t > 0)
    def _():
        pl.semaphore_signal(barrier, inc=1, device_id={"ta": t - 1}, device_id_type=MESH)

    @pl.when(t < nt - 1)
    def _():
        pl.semaphore_signal(barrier, inc=1, device_id={"ta": t + 1}, device_id_type=MESH)

    weights = []
    for i, (src, dst) in enumerate(((gate_hbm, w_gate), (up_hbm, w_up), (down_hbm, w_down))):
        load = pltpu.make_async_copy(src, dst, weight_sem.at[i])
        load.start()
        weights.append(load)

    for d in range(frames + 1):
        decay[d : d + 1, :] = jnp.exp(rate_ref[...] * (-float(d)))

    def norm_chunk(c):
        row_tiles = cols // ROWS

        def one(i):
            f = i // row_tiles
            rows = pl.ds(pl.multiple_of(c * cols + lax.rem(i, row_tiles) * ROWS, ROWS), ROWS)
            x = video[f, rows, :].astype(F32)
            scale = lax.rsqrt(jnp.mean(x * x, -1, keepdims=True) + EPS)
            normed[f, rows, :] = (x * scale).astype(BF16)

        loop(0, frames * row_tiles, one)

    def fwd_copy(p, c, slot_at_target):
        f, rows = place(p, c)
        return pltpu.make_async_remote_copy(
            src_ref=normed.at[f, rows],
            dst_ref=got.at[slot_at_target, pl.ds(c * part, part)],
            send_sem=fwd_send.at[c, p],
            recv_sem=fwd_recv.at[c, slot_at_target],
            device_id={"sa": p},
            device_id_type=MESH,
        )

    def back_copy(p, c, owner):
        f, rows = place(owner, c)
        return pltpu.make_async_remote_copy(
            src_ref=mixed.at[p, pl.ds(c * part, part)],
            dst_ref=back.at[f, rows],
            send_sem=back_send.at[c, p],
            recv_sem=back_recv.at[c, owner],
            device_id={"sa": p},
            device_id_type=MESH,
        )

    def halo_copy(c, up):
        dst = prev if up else after
        return pltpu.make_async_remote_copy(
            src_ref=normed.at[:, chunk_cols(c)],
            dst_ref=dst.at[:, chunk_cols(c)],
            send_sem=halo_send.at[c, int(up)],
            recv_sem=halo_recv.at[c, int(up)],
            device_id={"ta": t + 1 if up else t - 1},
            device_id_type=MESH,
        )

    for c in range(chunks):
        loads[c].wait()
        norm_chunk(c)
        if c == 0:
            greeted = (t > 0).astype(jnp.int32) + (t < nt - 1).astype(jnp.int32)
            pl.semaphore_wait(barrier, n - 1 + greeted)
        loop(1, n, lambda o, c=c: fwd_copy(lax.rem(me + o, n), c, me).start())

        @pl.when(t > 0)
        def _(c=c):
            halo_copy(c, False).start()

        @pl.when(t < nt - 1)
        def _(c=c):
            halo_copy(c, True).start()

    @pl.when(t == 0)
    def _():
        prev[...] = jnp.zeros_like(prev)

    @pl.when(t == nt - 1)
    def _():
        after[...] = jnp.zeros_like(after)

    def mix_chunk(c):
        own_f, own_rows = place(me, c)
        got[me, pl.ds(c * part, part), :] = normed[own_f, own_rows, :]

        def one(i):
            lanes = aligned(lax.rem(i, tiles), LANES)
            rows = pl.ds(pl.multiple_of(c * part + i // tiles * ROWS, ROWS), ROWS)
            if n <= 8:
                taps = [taps_ref[j, :, lanes] for j in range(2 * n - 1)]
                x = [got[k, rows, lanes].astype(F32) for k in range(n)]
                for h in range(n):
                    total = taps[h + n - 1] * x[0]
                    for k in range(1, n):
                        total = total + taps[h - k + n - 1] * x[k]
                    mixed[h, rows, lanes] = total.astype(BF16)
            else:
                def one_row(h):
                    def add(k, total):
                        tap = taps_ref[h - k + n - 1, :, lanes]
                        return total + tap * got[k, rows, lanes].astype(F32)

                    total = lax.fori_loop(0, n, add, jnp.zeros((ROWS, LANES), F32))
                    mixed[h, rows, lanes] = total.astype(BF16)

                loop(0, n, one_row)

        loop(0, part // ROWS * tiles, one)
        back[own_f, own_rows, :] = mixed[me, pl.ds(c * part, part), :]

    def time_chunk(c):
        last = frames - 1

        def one(i):
            lanes = aligned(lax.rem(i, tiles), LANES)
            rows = pl.ds(pl.multiple_of(c * cols + i // tiles * ROWS, ROWS), ROWS)
            a = [decay[d : d + 1, lanes] for d in range(frames + 1)]
            x = [normed[f, rows, lanes].astype(F32) for f in range(frames)]
            total = list(x)
            inner = jnp.zeros((ROWS, LANES), F32)
            for f in range(1, frames):
                inner = a[1] * (inner + x[f - 1])
                total[f] = total[f] + inner
            inner = jnp.zeros((ROWS, LANES), F32)
            for f in range(last - 1, -1, -1):
                inner = a[1] * (inner + x[f + 1])
                total[f] = total[f] + inner
            outer = jnp.zeros((ROWS, LANES), F32)
            for f in range(last, -1, -1):
                outer = outer + a[frames - f] * prev[f, rows, lanes].astype(F32)
                total[f] = total[f] + a[f] * outer
            outer = jnp.zeros((ROWS, LANES), F32)
            for f in range(frames):
                outer = outer + a[f + 1] * after[f, rows, lanes].astype(F32)
                total[f] = total[f] + a[last - f] * outer
            for f in range(frames):
                time_mix[f, rows, lanes] = total[f]

        loop(0, cols // ROWS * tiles, one)

    for c in range(chunks):
        loop(1, n, lambda o, c=c: fwd_copy(me, c, lax.rem(me + n - o, n)).wait_recv())
        mix_chunk(c)
        loop(1, n, lambda o, c=c: back_copy(lax.rem(me + o, n), c, me).start())

        @pl.when(t > 0)
        def _(c=c):
            halo_copy(c, True).wait_recv()

        @pl.when(t < nt - 1)
        def _(c=c):
            halo_copy(c, False).wait_recv()

        time_chunk(c)

    for load in weights:
        load.wait()

    block = max(256 // cols, 1)
    height = block * cols

    def feed_chunk(c):
        row_tiles = cols // ROWS

        def one(i):
            f = i // row_tiles
            rows = pl.ds(pl.multiple_of(c * cols + lax.rem(i, row_tiles) * ROWS, ROWS), ROWS)
            summed = (time_mix[f, rows, :] + back[f, rows, :].astype(F32)).astype(BF16)
            x = summed.astype(F32)
            scale = lax.rsqrt(jnp.mean(x * x, -1, keepdims=True) + EPS)
            normal[aligned(i, ROWS), :] = (x * scale * gain_ref[...]).astype(BF16)

        loop(0, frames * row_tiles, one)

        def blocks(b):
            flat = aligned(b, height)

            def widen(j):
                at = aligned(j, COLS)
                x = normal[flat, :]
                gate = jnp.dot(x, w_gate[:, at], preferred_element_type=F32)
                up = jnp.dot(x, w_up[:, at], preferred_element_type=F32)
                hidden[:, at] = (jax.nn.silu(gate) * up).astype(BF16)

            loop(0, w_gate.shape[1] // COLS, widen)

            def narrow(j):
                at = aligned(j, COLS)
                y = jnp.dot(hidden[...], w_down[:, at], preferred_element_type=F32)
                here = (pl.ds(b * block, block), chunk_cols(c), at)
                total = video[here].astype(F32) + y.reshape(block, cols, COLS)
                out[here] = total.astype(BF16)

            loop(0, channels // COLS, narrow)

        loop(0, frames // block, blocks)

    stores = []
    for c in range(chunks):
        loop(1, n, lambda o, c=c: back_copy(me, c, lax.rem(me + n - o, n)).wait_recv())
        feed_chunk(c)
        store = pltpu.make_async_copy(
            out.at[:, chunk_cols(c)], out_hbm.at[:, chunk_cols(c)], store_sem.at[c]
        )
        store.start()
        stores.append(store)

    for c in range(chunks):
        def sent(o, c=c):
            p = lax.rem(me + o, n)
            fwd_copy(p, c, me).wait_send()
            back_copy(p, c, me).wait_send()

        loop(1, n, sent)

        @pl.when(t > 0)
        def _(c=c):
            halo_copy(c, False).wait_send()

        @pl.when(t < nt - 1)
        def _(c=c):
            halo_copy(c, True).wait_send()

        stores[c].wait()


def body(n, nt, video, mix_gain, t_rate, s_kernel, w_gate, w_up, w_down):
    frames, _, width, channels = video.shape
    hid = w_gate.shape[1]
    group = frames * width // n
    chunks = 4 if group == width else 1
    cols = width // chunks
    height = max(256 // cols, 1) * cols
    clip = (frames, width, channels)
    sem = pltpu.SemaphoreType.DMA
    vmem = pl.BlockSpec(memory_space=pltpu.VMEM)
    hbm = pl.BlockSpec(memory_space=pl.ANY)
    tokens = frames * width
    result = pl.pallas_call(
        functools.partial(kernel, n, nt, chunks),
        out_shape=jax.ShapeDtypeStruct(clip, BF16),
        in_specs=[hbm, vmem, vmem, vmem, hbm, hbm, hbm],
        out_specs=hbm,
        scratch_shapes=[
            pltpu.VMEM(clip, BF16),
            pltpu.VMEM(clip, BF16),
            pltpu.VMEM(clip, BF16),
            pltpu.VMEM(clip, BF16),
            pltpu.VMEM((n, group, channels), BF16),
            pltpu.VMEM((n, group, channels), BF16),
            pltpu.VMEM(clip, BF16),
            pltpu.VMEM(clip, F32),
            pltpu.VMEM((frames * cols, channels), BF16),
            pltpu.VMEM((height, hid), BF16),
            pltpu.VMEM(clip, BF16),
            pltpu.VMEM((channels, hid), BF16),
            pltpu.VMEM((channels, hid), BF16),
            pltpu.VMEM((hid, channels), BF16),
            pltpu.VMEM((frames + 8, channels), F32),
            sem((chunks,)),
            sem((3,)),
            sem((chunks,)),
            sem((chunks, n)),
            sem((chunks, n)),
            sem((chunks, n)),
            sem((chunks, n)),
            sem((chunks, 2)),
            sem((chunks, 2)),
        ],
        compiler_params=pltpu.CompilerParams(
            collective_id=0, has_side_effects=True, vmem_limit_bytes=52 * 2**20
        ),
        cost_estimate=pl.CostEstimate(
            flops=6 * tokens * channels * hid,
            bytes_accessed=4 * tokens * channels + 6 * channels * hid,
            transcendentals=tokens * hid,
        ),
    )(
        video.reshape(clip),
        mix_gain.reshape(1, channels),
        t_rate.reshape(1, channels),
        s_kernel.reshape(-1, 1, channels),
        w_gate,
        w_up,
        w_down,
    )
    return result.reshape(video.shape)


def solution(mesh):
    in_specs = (P("ta", "sa", None, None), P(), P(), P(), P(), P(), P())
    return jax.shard_map(
        functools.partial(body, mesh.shape["sa"], mesh.shape["ta"]),
        mesh=mesh,
        in_specs=in_specs,
        out_specs=P("ta", "sa", None, None),
        check_vma=False,
    )
```

```python
import functools

import jax
import jax.numpy as jnp
from jax import lax
from jax.experimental import pallas as pl
from jax.experimental.pallas import tpu as pltpu
from jax.sharding import PartitionSpec as P

EPS = 1e-06
MESH = pl.DeviceIdType.MESH
ROWS = 16
LANES = 128
COLS = 256
F32 = jnp.float32
BF16 = jnp.bfloat16


def loop(start, stop, step_fn):
    def step(i, carry):
        step_fn(i)
        return carry

    lax.fori_loop(start, stop, step, 0)


def aligned(index, size):
    return pl.ds(pl.multiple_of(index * size, size), size)


def kernel(
    n, nt, pieces,
    video_hbm, gain_hbm, rate_hbm, taps_hbm, gate_hbm, up_hbm, down_hbm,
    out,
    video, normed, prev, after, got, mixed, back, time_mix, normal, hidden,
    gain_ref, rate_ref, taps_ref, w_gate, w_up, w_down, decay,
    load_sem, small_sem, weight_sem,
    fwd_send, fwd_recv, back_send, back_recv, halo_send, halo_recv,
):
    frames, width, channels = video.shape
    group = frames * width // n
    chunks = len(pieces)
    me = lax.axis_index("sa")
    t = lax.axis_index("ta")
    per_frame = width // group
    tiles = channels // LANES

    def chunk_cols(c):
        return pl.ds(*pieces[c])

    def chunk_part(c):
        return pl.ds(pieces[c][0] * group // width, pieces[c][1] * group // width)

    def peer(o):
        p, bit = me, 1
        while bit < n:
            p = p + lax.rem(o // bit, 2) * (1 - 2 * lax.rem(me // bit, 2)) * bit
            bit *= 2
        return p

    def each_peer(step_fn):
        loop(1, n, lambda i: step_fn(peer(n - i)))

    def place(p, c):
        rows = chunk_part(c)
        start = lax.rem(p, per_frame) * group + rows.start
        return p // per_frame, pl.ds(pl.multiple_of(start, ROWS), rows.size)

    smalls = []
    for i, (src, dst) in enumerate(
        ((rate_hbm, rate_ref), (taps_hbm, taps_ref), (gain_hbm, gain_ref))
    ):
        smalls.append(pltpu.make_async_copy(src, dst, small_sem.at[i]))
    loads = []
    for c in range(chunks):
        load = pltpu.make_async_copy(
            video_hbm.at[:, chunk_cols(c)], video.at[:, chunk_cols(c)], load_sem.at[c]
        )
        load.start()
        loads.append(load)

    for load in smalls:
        load.start()

    barrier = pltpu.get_barrier_semaphore()

    def greet(p):
        pl.semaphore_signal(barrier, inc=1, device_id={"sa": p}, device_id_type=MESH)

    each_peer(greet)

    @pl.when(t > 0)
    def _():
        pl.semaphore_signal(barrier, inc=1, device_id={"ta": t - 1}, device_id_type=MESH)

    @pl.when(t < nt - 1)
    def _():
        pl.semaphore_signal(barrier, inc=1, device_id={"ta": t + 1}, device_id_type=MESH)

    weights = []
    for i, (src, dst) in enumerate(((gate_hbm, w_gate), (up_hbm, w_up), (down_hbm, w_down))):
        load = pltpu.make_async_copy(src, dst, weight_sem.at[i])
        load.start()
        weights.append(load)

    def norm_chunk(c):
        first, cols = pieces[c]
        row_tiles = cols // ROWS

        def one(i):
            f = i // row_tiles
            rows = pl.ds(pl.multiple_of(first + lax.rem(i, row_tiles) * ROWS, ROWS), ROWS)
            x = video[f, rows, :].astype(F32)
            scale = lax.rsqrt(jnp.mean(x * x, -1, keepdims=True) + EPS)
            normed[f, rows, :] = (x * scale).astype(BF16)

        loop(0, frames * row_tiles, one)

    def fwd_copy(p, c, slot_at_target):
        f, rows = place(p, c)
        return pltpu.make_async_remote_copy(
            src_ref=normed.at[f, rows],
            dst_ref=got.at[slot_at_target, chunk_part(c)],
            send_sem=fwd_send.at[c, p],
            recv_sem=fwd_recv.at[c, slot_at_target],
            device_id={"sa": p},
            device_id_type=MESH,
        )

    def back_copy(p, c, owner):
        f, rows = place(owner, c)
        return pltpu.make_async_remote_copy(
            src_ref=mixed.at[p, chunk_part(c)],
            dst_ref=back.at[f, rows],
            send_sem=back_send.at[c, p],
            recv_sem=back_recv.at[c, owner],
            device_id={"sa": p},
            device_id_type=MESH,
        )

    def halo_copy(c, up):
        dst = prev if up else after
        return pltpu.make_async_remote_copy(
            src_ref=normed.at[:, chunk_cols(c)],
            dst_ref=dst.at[:, chunk_cols(c)],
            send_sem=halo_send.at[c, int(up)],
            recv_sem=halo_recv.at[c, int(up)],
            device_id={"ta": t + 1 if up else t - 1},
            device_id_type=MESH,
        )

    for c in range(chunks):
        loads[c].wait()
        norm_chunk(c)
        if c == 0:
            greeted = (t > 0).astype(jnp.int32) + (t < nt - 1).astype(jnp.int32)
            pl.semaphore_wait(barrier, n - 1 + greeted)
        each_peer(lambda p, c=c: fwd_copy(p, c, me).start())

        @pl.when(t > 0)
        def _(c=c):
            halo_copy(c, False).start()

        @pl.when(t < nt - 1)
        def _(c=c):
            halo_copy(c, True).start()

    for load in smalls:
        load.wait()

    for d in range(frames + 1):
        decay[d : d + 1, :] = jnp.exp(rate_ref[...] * (-float(d)))

    @pl.when(t == 0)
    def _():
        prev[...] = jnp.zeros_like(prev)

    @pl.when(t == nt - 1)
    def _():
        after[...] = jnp.zeros_like(after)

    def mix_chunk(c):
        own_f, own_rows = place(me, c)
        part = chunk_part(c)
        got[me, part, :] = normed[own_f, own_rows, :]

        def one(i):
            lanes = aligned(lax.rem(i, tiles), LANES)
            rows = pl.ds(pl.multiple_of(part.start + i // tiles * ROWS, ROWS), ROWS)
            if n <= 8:
                taps = [taps_ref[j : j + 1, lanes] for j in range(2 * n - 1)]
                x = [got[k, rows, lanes].astype(F32) for k in range(n)]
                for h in range(n):
                    total = taps[h + n - 1] * x[0]
                    for k in range(1, n):
                        total = total + taps[h - k + n - 1] * x[k]
                    mixed[h, rows, lanes] = total.astype(BF16)
            else:
                def one_row(h):
                    def add(k, total):
                        tap = taps_ref[h - k + n - 1, :, lanes]
                        return total + tap * got[k, rows, lanes].astype(F32)

                    total = lax.fori_loop(0, n, add, jnp.zeros((ROWS, LANES), F32))
                    mixed[h, rows, lanes] = total.astype(BF16)

                loop(0, n, one_row)

        loop(0, part.size // ROWS * tiles, one)
        back[own_f, own_rows, :] = mixed[me, part, :]

    def time_chunk(c):
        last = frames - 1
        first, cols = pieces[c]

        def one(i):
            lanes = aligned(lax.rem(i, tiles), LANES)
            rows = pl.ds(pl.multiple_of(first + i // tiles * ROWS, ROWS), ROWS)
            a = [decay[d : d + 1, lanes] for d in range(frames + 1)]
            x = [normed[f, rows, lanes].astype(F32) for f in range(frames)]
            total = list(x)
            inner = jnp.zeros((ROWS, LANES), F32)
            for f in range(1, frames):
                inner = a[1] * (inner + x[f - 1])
                total[f] = total[f] + inner
            inner = jnp.zeros((ROWS, LANES), F32)
            for f in range(last - 1, -1, -1):
                inner = a[1] * (inner + x[f + 1])
                total[f] = total[f] + inner
            outer = jnp.zeros((ROWS, LANES), F32)
            for f in range(last, -1, -1):
                outer = outer + a[frames - f] * prev[f, rows, lanes].astype(F32)
                total[f] = total[f] + a[f] * outer
            outer = jnp.zeros((ROWS, LANES), F32)
            for f in range(frames):
                outer = outer + a[f + 1] * after[f, rows, lanes].astype(F32)
                total[f] = total[f] + a[last - f] * outer
            for f in range(frames):
                time_mix[f, rows, lanes] = total[f]

        loop(0, cols // ROWS * tiles, one)

    for c in range(chunks):
        each_peer(lambda p, c=c: fwd_copy(p, c, p).wait_recv())
        mix_chunk(c)
        each_peer(lambda p, c=c: back_copy(p, c, me).start())

        @pl.when(t > 0)
        def _(c=c):
            halo_copy(c, True).wait_recv()

        @pl.when(t < nt - 1)
        def _(c=c):
            halo_copy(c, False).wait_recv()

        time_chunk(c)

    for load in weights:
        load.wait()

    def feed_chunk(c):
        first, cols = pieces[c]
        row_tiles = cols // ROWS

        def one(i):
            f = i // row_tiles
            rows = pl.ds(pl.multiple_of(first + lax.rem(i, row_tiles) * ROWS, ROWS), ROWS)
            summed = (time_mix[f, rows, :] + back[f, rows, :].astype(F32)).astype(BF16)
            x = summed.astype(F32)
            scale = lax.rsqrt(jnp.mean(x * x, -1, keepdims=True) + EPS)
            normal[aligned(i, ROWS), :] = (x * scale * gain_ref[...]).astype(BF16)

        loop(0, frames * row_tiles, one)

        block = min(max(256 // cols, 1), frames)
        height = block * cols

        def blocks(b):
            flat = aligned(b, height)

            def widen(j):
                at = aligned(j, COLS)
                x = normal[flat, :]
                gate = jnp.dot(x, w_gate[:, at], preferred_element_type=F32)
                up = jnp.dot(x, w_up[:, at], preferred_element_type=F32)
                hidden[:height, at] = (jax.nn.silu(gate) * up).astype(BF16)

            loop(0, w_gate.shape[1] // COLS, widen)

            def narrow(j):
                at = aligned(j, COLS)
                y = jnp.dot(hidden[:height, :], w_down[:, at], preferred_element_type=F32)
                here = (pl.ds(b * block, block), chunk_cols(c), at)
                total = video[here].astype(F32) + y.reshape(block, cols, COLS)
                out[here] = total.astype(BF16)

            loop(0, channels // COLS, narrow)

        loop(0, frames // block, blocks)

    for c in range(chunks):
        each_peer(lambda p, c=c: back_copy(p, c, p).wait_recv())
        feed_chunk(c)

    for c in range(chunks):
        def sent(p, c=c):
            fwd_copy(p, c, me).wait_send()
            back_copy(p, c, me).wait_send()

        each_peer(sent)

        @pl.when(t > 0)
        def _(c=c):
            halo_copy(c, False).wait_send()

        @pl.when(t < nt - 1)
        def _(c=c):
            halo_copy(c, True).wait_send()


def body(n, nt, video, mix_gain, t_rate, s_kernel, w_gate, w_up, w_down):
    frames, _, width, channels = video.shape
    hid = w_gate.shape[1]
    group = frames * width // n
    eighths = [1, 2, 2, 2, 1] if group == width else [8]
    sizes = [width * e // 8 for e in eighths]
    chunks = len(sizes)
    pieces = [(sum(sizes[:c]), sizes[c]) for c in range(chunks)]
    most = max(sizes)
    height = min(max(256 // most, 1), frames) * most
    taps = s_kernel if n <= 8 else s_kernel.reshape(-1, 1, channels)
    clip = (frames, width, channels)
    sem = pltpu.SemaphoreType.DMA
    hbm = pl.BlockSpec(memory_space=pltpu.HBM)
    tokens = frames * width
    result = pl.pallas_call(
        functools.partial(kernel, n, nt, pieces),
        out_shape=jax.ShapeDtypeStruct(clip, BF16),
        in_specs=[hbm] * 7,
        out_specs=pl.BlockSpec(memory_space=pltpu.VMEM),
        scratch_shapes=[
            pltpu.VMEM(clip, BF16),
            pltpu.VMEM(clip, BF16),
            pltpu.VMEM(clip, BF16),
            pltpu.VMEM(clip, BF16),
            pltpu.VMEM((n, group, channels), BF16),
            pltpu.VMEM((n, group, channels), BF16),
            pltpu.VMEM(clip, BF16),
            pltpu.VMEM(clip, F32),
            pltpu.VMEM((frames * most, channels), BF16),
            pltpu.VMEM((height, hid), BF16),
            pltpu.VMEM((1, channels), F32),
            pltpu.VMEM((1, channels), F32),
            pltpu.VMEM(taps.shape, F32),
            pltpu.VMEM((channels, hid), BF16),
            pltpu.VMEM((channels, hid), BF16),
            pltpu.VMEM((hid, channels), BF16),
            pltpu.VMEM((frames + 8, channels), F32),
            sem((chunks,)),
            sem((3,)),
            sem((3,)),
            sem((chunks, n)),
            sem((chunks, n)),
            sem((chunks, n)),
            sem((chunks, n)),
            sem((chunks, 2)),
            sem((chunks, 2)),
        ],
        compiler_params=pltpu.CompilerParams(
            collective_id=0, has_side_effects=True, vmem_limit_bytes=60 * 2**20
        ),
        cost_estimate=pl.CostEstimate(
            flops=6 * tokens * channels * hid,
            bytes_accessed=4 * tokens * channels + 6 * channels * hid,
            transcendentals=tokens * hid,
        ),
    )(
        video.reshape(clip),
        mix_gain.reshape(1, channels),
        t_rate.reshape(1, channels),
        taps,
        w_gate,
        w_up,
        w_down,
    )
    return result.reshape(video.shape)


def solution(mesh):
    in_specs = (P("ta", "sa", None, None), P(), P(), P(), P(), P(), P())
    return jax.shard_map(
        functools.partial(body, mesh.shape["sa"], mesh.shape["ta"]),
        mesh=mesh,
        in_specs=in_specs,
        out_specs=P("ta", "sa", None, None),
        check_vma=False,
    )
```

```python
import functools

import jax
import jax.numpy as jnp
from jax import lax
from jax.experimental import pallas as pl
from jax.experimental.pallas import tpu as pltpu
from jax.sharding import PartitionSpec as P

EPS = 1e-06
MESH = pl.DeviceIdType.MESH
ROWS = 16
LANES = 128
COLS = 256
F32 = jnp.float32
BF16 = jnp.bfloat16


def loop(start, stop, step_fn):
    def step(i, carry):
        step_fn(i)
        return carry

    lax.fori_loop(start, stop, step, 0)


def aligned(index, size):
    return pl.ds(pl.multiple_of(index * size, size), size)


def kernel(
    n, nt, pieces,
    video_hbm, gain_hbm, rate_hbm, taps_hbm, gate_hbm, up_hbm, down_hbm,
    out,
    video, normed, prev, after, got, mixed, back, time_mix, normal, hidden,
    gain_ref, rate_ref, taps_ref, w_gate, w_up, w_down, decay,
    load_sem, small_sem, weight_sem,
    fwd_send, fwd_recv, back_send, back_recv, halo_send, halo_recv,
):
    frames, width, channels = video.shape
    group = frames * width // n
    chunks = len(pieces)
    me = lax.axis_index("sa")
    t = lax.axis_index("ta")
    per_frame = width // group
    tiles = channels // LANES

    def chunk_cols(c):
        return pl.ds(*pieces[c])

    def chunk_part(c):
        return pl.ds(pieces[c][0] * group // width, pieces[c][1] * group // width)

    def peer(o):
        p = lax.rem(me + n - o, n)
        return p

    def each_peer(step_fn):
        loop(1, n, lambda i: step_fn(peer(n - i)))

    def place(p, c):
        rows = chunk_part(c)
        start = lax.rem(p, per_frame) * group + rows.start
        return p // per_frame, pl.ds(pl.multiple_of(start, ROWS), rows.size)

    smalls = []
    for i, (src, dst) in enumerate(
        ((rate_hbm, rate_ref), (taps_hbm, taps_ref), (gain_hbm, gain_ref))
    ):
        smalls.append(pltpu.make_async_copy(src, dst, small_sem.at[i]))
    loads = []
    for c in range(chunks):
        load = pltpu.make_async_copy(
            video_hbm.at[:, chunk_cols(c)], video.at[:, chunk_cols(c)], load_sem.at[c]
        )
        load.start()
        loads.append(load)

    for load in smalls:
        load.start()

    barrier = pltpu.get_barrier_semaphore()

    def greet(p):
        pl.semaphore_signal(barrier, inc=1, device_id={"sa": p}, device_id_type=MESH)

    each_peer(greet)

    @pl.when(t > 0)
    def _():
        pl.semaphore_signal(barrier, inc=1, device_id={"ta": t - 1}, device_id_type=MESH)

    @pl.when(t < nt - 1)
    def _():
        pl.semaphore_signal(barrier, inc=1, device_id={"ta": t + 1}, device_id_type=MESH)

    weights = []
    for i, (src, dst) in enumerate(((gate_hbm, w_gate), (up_hbm, w_up), (down_hbm, w_down))):
        load = pltpu.make_async_copy(src, dst, weight_sem.at[i])
        load.start()
        weights.append(load)

    def norm_chunk(c):
        first, cols = pieces[c]
        row_tiles = cols // ROWS

        def one(i):
            f = i // row_tiles
            rows = pl.ds(pl.multiple_of(first + lax.rem(i, row_tiles) * ROWS, ROWS), ROWS)
            x = video[f, rows, :].astype(F32)
            scale = lax.rsqrt(jnp.mean(x * x, -1, keepdims=True) + EPS)
            normed[f, rows, :] = (x * scale).astype(BF16)

        loop(0, frames * row_tiles, one)

    def fwd_copy(p, c, slot_at_target):
        f, rows = place(p, c)
        return pltpu.make_async_remote_copy(
            src_ref=normed.at[f, rows],
            dst_ref=got.at[slot_at_target, chunk_part(c)],
            send_sem=fwd_send.at[c, p],
            recv_sem=fwd_recv.at[c, slot_at_target],
            device_id={"sa": p},
            device_id_type=MESH,
        )

    def back_copy(p, c, owner):
        f, rows = place(owner, c)
        return pltpu.make_async_remote_copy(
            src_ref=mixed.at[p, chunk_part(c)],
            dst_ref=back.at[f, rows],
            send_sem=back_send.at[c, p],
            recv_sem=back_recv.at[c, owner],
            device_id={"sa": p},
            device_id_type=MESH,
        )

    def halo_copy(c, up):
        dst = prev if up else after
        return pltpu.make_async_remote_copy(
            src_ref=normed.at[:, chunk_cols(c)],
            dst_ref=dst.at[:, chunk_cols(c)],
            send_sem=halo_send.at[c, int(up)],
            recv_sem=halo_recv.at[c, int(up)],
            device_id={"ta": t + 1 if up else t - 1},
            device_id_type=MESH,
        )

    for c in range(chunks):
        loads[c].wait()
        norm_chunk(c)
        if c == 0:
            greeted = (t > 0).astype(jnp.int32) + (t < nt - 1).astype(jnp.int32)
            pl.semaphore_wait(barrier, n - 1 + greeted)
        each_peer(lambda p, c=c: fwd_copy(p, c, me).start())

        @pl.when(t > 0)
        def _(c=c):
            halo_copy(c, False).start()

        @pl.when(t < nt - 1)
        def _(c=c):
            halo_copy(c, True).start()

    for load in smalls:
        load.wait()

    for d in range(frames + 1):
        decay[d : d + 1, :] = jnp.exp(rate_ref[...] * (-float(d)))

    @pl.when(t == 0)
    def _():
        prev[...] = jnp.zeros_like(prev)

    @pl.when(t == nt - 1)
    def _():
        after[...] = jnp.zeros_like(after)

    def mix_chunk(c):
        own_f, own_rows = place(me, c)
        part = chunk_part(c)
        got[me, part, :] = normed[own_f, own_rows, :]

        def one(i):
            lanes = aligned(lax.rem(i, tiles), LANES)
            rows = pl.ds(pl.multiple_of(part.start + i // tiles * ROWS, ROWS), ROWS)
            if n <= 8:
                taps = [taps_ref[j : j + 1, lanes] for j in range(2 * n - 1)]
                x = [got[k, rows, lanes].astype(F32) for k in range(n)]
                for h in range(n):
                    total = taps[h + n - 1] * x[0]
                    for k in range(1, n):
                        total = total + taps[h - k + n - 1] * x[k]
                    mixed[h, rows, lanes] = total.astype(BF16)
            else:
                def one_row(h):
                    def add(k, total):
                        tap = taps_ref[h - k + n - 1, :, lanes]
                        return total + tap * got[k, rows, lanes].astype(F32)

                    total = lax.fori_loop(0, n, add, jnp.zeros((ROWS, LANES), F32))
                    mixed[h, rows, lanes] = total.astype(BF16)

                loop(0, n, one_row)

        loop(0, part.size // ROWS * tiles, one)
        back[own_f, own_rows, :] = mixed[me, part, :]

    def time_chunk(c):
        last = frames - 1
        first, cols = pieces[c]

        def one(i):
            lanes = aligned(lax.rem(i, tiles), LANES)
            rows = pl.ds(pl.multiple_of(first + i // tiles * ROWS, ROWS), ROWS)
            a = [decay[d : d + 1, lanes] for d in range(frames + 1)]
            x = [normed[f, rows, lanes].astype(F32) for f in range(frames)]
            total = list(x)
            inner = jnp.zeros((ROWS, LANES), F32)
            for f in range(1, frames):
                inner = a[1] * (inner + x[f - 1])
                total[f] = total[f] + inner
            inner = jnp.zeros((ROWS, LANES), F32)
            for f in range(last - 1, -1, -1):
                inner = a[1] * (inner + x[f + 1])
                total[f] = total[f] + inner
            outer = jnp.zeros((ROWS, LANES), F32)
            for f in range(last, -1, -1):
                outer = outer + a[frames - f] * prev[f, rows, lanes].astype(F32)
                total[f] = total[f] + a[f] * outer
            outer = jnp.zeros((ROWS, LANES), F32)
            for f in range(frames):
                outer = outer + a[f + 1] * after[f, rows, lanes].astype(F32)
                total[f] = total[f] + a[last - f] * outer
            for f in range(frames):
                time_mix[f, rows, lanes] = total[f]

        loop(0, cols // ROWS * tiles, one)

    for c in range(chunks):
        each_peer(lambda p, c=c: fwd_copy(p, c, p).wait_recv())
        mix_chunk(c)
        each_peer(lambda p, c=c: back_copy(p, c, me).start())

        @pl.when(t > 0)
        def _(c=c):
            halo_copy(c, True).wait_recv()

        @pl.when(t < nt - 1)
        def _(c=c):
            halo_copy(c, False).wait_recv()

        time_chunk(c)

    for load in weights:
        load.wait()

    def feed_chunk(c):
        first, cols = pieces[c]
        row_tiles = cols // ROWS

        def one(i):
            f = i // row_tiles
            rows = pl.ds(pl.multiple_of(first + lax.rem(i, row_tiles) * ROWS, ROWS), ROWS)
            summed = (time_mix[f, rows, :] + back[f, rows, :].astype(F32)).astype(BF16)
            x = summed.astype(F32)
            scale = lax.rsqrt(jnp.mean(x * x, -1, keepdims=True) + EPS)
            normal[aligned(i, ROWS), :] = (x * scale * gain_ref[...]).astype(BF16)

        loop(0, frames * row_tiles, one)

        block = min(max(256 // cols, 1), frames)
        height = block * cols

        def blocks(b):
            flat = aligned(b, height)

            def widen(j):
                at = aligned(j, COLS)
                x = normal[flat, :]
                gate = jnp.dot(x, w_gate[:, at], preferred_element_type=F32)
                up = jnp.dot(x, w_up[:, at], preferred_element_type=F32)
                hidden[:height, at] = (jax.nn.silu(gate) * up).astype(BF16)

            loop(0, w_gate.shape[1] // COLS, widen)

            def narrow(j):
                at = aligned(j, COLS)
                y = jnp.dot(hidden[:height, :], w_down[:, at], preferred_element_type=F32)
                here = (pl.ds(b * block, block), chunk_cols(c), at)
                total = video[here].astype(F32) + y.reshape(block, cols, COLS)
                out[here] = total.astype(BF16)

            loop(0, channels // COLS, narrow)

        loop(0, frames // block, blocks)

    for c in range(chunks):
        each_peer(lambda p, c=c: back_copy(p, c, p).wait_recv())
        feed_chunk(c)

    for c in range(chunks):
        def sent(p, c=c):
            fwd_copy(p, c, me).wait_send()
            back_copy(p, c, me).wait_send()

        each_peer(sent)

        @pl.when(t > 0)
        def _(c=c):
            halo_copy(c, False).wait_send()

        @pl.when(t < nt - 1)
        def _(c=c):
            halo_copy(c, True).wait_send()


def body(n, nt, video, mix_gain, t_rate, s_kernel, w_gate, w_up, w_down):
    frames, _, width, channels = video.shape
    hid = w_gate.shape[1]
    group = frames * width // n
    eighths = [2, 2, 2, 2] if group == width else [8]
    sizes = [width * e // 8 for e in eighths]
    chunks = len(sizes)
    pieces = [(sum(sizes[:c]), sizes[c]) for c in range(chunks)]
    most = max(sizes)
    height = min(max(256 // most, 1), frames) * most
    taps = s_kernel if n <= 8 else s_kernel.reshape(-1, 1, channels)
    clip = (frames, width, channels)
    sem = pltpu.SemaphoreType.DMA
    hbm = pl.BlockSpec(memory_space=pltpu.HBM)
    tokens = frames * width
    result = pl.pallas_call(
        functools.partial(kernel, n, nt, pieces),
        out_shape=jax.ShapeDtypeStruct(clip, BF16),
        in_specs=[hbm] * 7,
        out_specs=pl.BlockSpec(memory_space=pltpu.VMEM),
        scratch_shapes=[
            pltpu.VMEM(clip, BF16),
            pltpu.VMEM(clip, BF16),
            pltpu.VMEM(clip, BF16),
            pltpu.VMEM(clip, BF16),
            pltpu.VMEM((n, group, channels), BF16),
            pltpu.VMEM((n, group, channels), BF16),
            pltpu.VMEM(clip, BF16),
            pltpu.VMEM(clip, F32),
            pltpu.VMEM((frames * most, channels), BF16),
            pltpu.VMEM((height, hid), BF16),
            pltpu.VMEM((1, channels), F32),
            pltpu.VMEM((1, channels), F32),
            pltpu.VMEM(taps.shape, F32),
            pltpu.VMEM((channels, hid), BF16),
            pltpu.VMEM((channels, hid), BF16),
            pltpu.VMEM((hid, channels), BF16),
            pltpu.VMEM((frames + 8, channels), F32),
            sem((chunks,)),
            sem((3,)),
            sem((3,)),
            sem((chunks, n)),
            sem((chunks, n)),
            sem((chunks, n)),
            sem((chunks, n)),
            sem((chunks, 2)),
            sem((chunks, 2)),
        ],
        compiler_params=pltpu.CompilerParams(
            collective_id=0, has_side_effects=True, vmem_limit_bytes=60 * 2**20
        ),
        cost_estimate=pl.CostEstimate(
            flops=6 * tokens * channels * hid,
            bytes_accessed=4 * tokens * channels + 6 * channels * hid,
            transcendentals=tokens * hid,
        ),
    )(
        video.reshape(clip),
        mix_gain.reshape(1, channels),
        t_rate.reshape(1, channels),
        taps,
        w_gate,
        w_up,
        w_down,
    )
    return result.reshape(video.shape)


def solution(mesh):
    in_specs = (P("ta", "sa", None, None), P(), P(), P(), P(), P(), P())
    return jax.shard_map(
        functools.partial(body, mesh.shape["sa"], mesh.shape["ta"]),
        mesh=mesh,
        in_specs=in_specs,
        out_specs=P("ta", "sa", None, None),
        check_vma=False,
    )
```
